768 devices in a mesh: outer: 96 (over z, x, core), node: 8 (over y).
Axes of the slice: x: 4, y: 8, z: 12, core: 2. Of those that a mesh axis runs over, the one named last changes fastest.
Arguments:
- bag_grads: float32 [24576, 128], P(('outer', 'node')), may hold values from -6 to 6
- bag_lengths: int32 [768, 32], P(('outer', 'node')), may hold values from 1 to 32, 512 in all within a row
- look_slot: int32 [768, 512], P(('outer', 'node')), may hold values from 0 to 191, as said below
- group_slot: int32 [768, 8, 24], P(('outer', 'node')), may hold values from 0 to 191, as said below
- owner_row: int32 [768, 96, 2], P(('outer', 'node')), may hold values from 0 to 1023, as said below
- table: float32 [786432, 128], P(('outer', 'node')), may hold values from -3 to 3
- accum: float32 [786432], P(('outer', 'node')), may hold values from 0.5 to 4
Outputs:
- new_table: float32 [786432, 128], P(('outer', 'node'))
- new_accum: float32 [786432], P(('outer', 'node'))
- fresh_rows: bfloat16 [393216, 128], P(('outer', 'node'))
The draws below stay inside these ranges and needn't reach their ends.
Inputs may be any that keep to these rules, and one draw needn't show every extreme that they name: `look_slot`: entry m * 24 + c is slot c of the block for node peer m; two lookups of one device share a slot exactly when they read the same table row. `group_slot`: entry u * 2 + k is slot k of the block for outer peer u; the entries of one device for one sending peer n are distinct; slots that carry no lookup name an arbitrary entry. `owner_row`: within one device and one sending peer the rows of different slots differ; slots that carry no lookup name an arbitrary row.
All inputs are finite; a program needn't handle non-finite values.
Results may differ from the reference program's by a relative error of at most 0.001.
Values may be sent and summed in bfloat16 or wider, within the bound.
A program may use at most 32 MiB of HBM per device.

```python
import math
import jax
import jax.numpy as jnp
import numpy as np
from jax import lax

E = 128
ROWS_DEV = 1024
LOOK_DEV = 512
POOL = 16
CAP2 = 2
G = 96
M = 8
BAG_DEV = 32
CAP1 = 24


def draw_look_slot(key, part):
    key = jax.random.fold_in(key, 11)
    key_perm, key_extra, key_pick = jax.random.split(key, 3)
    devices = G * M
    span_slots = M * CAP1
    shuffled = jax.vmap(lambda one_key: jax.random.permutation(one_key, LOOK_DEV))(jax.random.split(key_perm, devices)) % span_slots
    random_slot = jax.random.randint(key_extra, (devices, LOOK_DEV), 0, span_slots)
    replace = jax.random.randint(key_pick, (devices, LOOK_DEV), 0, 4) == 0
    return jnp.where(replace, random_slot, shuffled).astype(jnp.int32)


def draw_group_slot(key, part):
    key = jax.random.fold_in(key, 23)
    key_base, key_own = jax.random.split(key, 2)
    devices = G * M
    span_slots = G * CAP2
    base = jax.vmap(lambda one_key: jax.random.permutation(one_key, span_slots))(jax.random.split(key_base, devices))
    base = base.reshape(devices, M, CAP1)
    own = jax.vmap(lambda one_key: jax.random.permutation(one_key, span_slots)[:CAP1])(jax.random.split(key_own, devices * M))
    own = own.reshape(devices, M, CAP1)
    senders = jnp.arange(M, dtype=jnp.int32)
    apart = senders >= 3 * M // 4
    return jnp.where(apart[None, :, None], own, base).astype(jnp.int32)


def draw_owner_row(key, part):
    key = jax.random.fold_in(key, 37)
    key_hot, key_cold, key_pick = jax.random.split(key, 3)
    full_shape = (G * M, G, CAP2)
    span_rows = ROWS_DEV // CAP2
    hot_rows = jax.random.randint(key_hot, full_shape, 0, 8)
    cold_rows = jax.random.randint(key_cold, full_shape, 0, span_rows)
    replace = jax.random.randint(key_pick, full_shape, 0, 2) == 0
    offsets = jnp.arange(CAP2, dtype=jnp.int32) * span_rows
    return (offsets[None, None, :] + jnp.where(replace, hot_rows, cold_rows)).astype(jnp.int32)


def block_scale(rng, extent, shards, low, largest):
    def one(dim, blocks):
        steps = jax.random.uniform(jax.random.fold_in(jax.random.fold_in(rng, 6), dim), (blocks,), jnp.float32, low / len(shards), largest / len(shards))
        return jnp.repeat(jnp.exp(steps), extent[dim] // blocks).reshape((-1,) + (1,) * (len(extent) - dim - 1))

    level = one(*shards[0])
    for cut in shards[1:]:
        level = level * one(*cut)
    return level


def profile(count, total, reach, skew):
    weights = [(1 << 20) // math.isqrt(grade ** skew) + 1 for grade in range(2, count + 1)]
    surplus, given = total - reach - (count - 1), [1] * (count - 1)
    while surplus > 0:
        free = [i for i in range(count - 1) if given[i] < reach]
        whole, left = sum([weights[i] for i in free]), surplus
        for i in free:
            extra = min(reach - given[i], max(1, left * weights[i] // whole), surplus)
            given[i] = given[i] + extra
            surplus = surplus - extra
    return np.array([reach] + given)


def ragged_sizes(own_key, amount, total, reach, slope):
    if amount == 2:
        one = jax.random.randint(own_key, (), max(1, total - reach), min(reach, total - 1) + 1)
        return jnp.stack([one, total - one])
    sizes = jnp.asarray(profile(amount, total, reach, slope), jnp.int32)
    pairs = (amount - 1) // 2
    giver, sink = sizes[1:1 + 2 * pairs:2], sizes[2:2 + 2 * pairs:2]
    margin = jnp.minimum(giver - 1, reach - sink)
    shifted = jax.random.randint(jax.random.fold_in(own_key, 1), (pairs,), 0, 1 << 20) % (margin + 1)
    sizes = sizes.at[1:1 + 2 * pairs:2].set(giver - shifted).at[2:2 + 2 * pairs:2].set(sink + shifted)
    return sizes[jax.random.permutation(jax.random.fold_in(own_key, 2), amount)]


def scatter_about(key, extent, width, reach, shards=(), held_as=jnp.bfloat16):
    loudness = block_scale(key, extent, shards, -0.22, 0.18) if shards else 1.0
    drawn = jax.random.normal(key, extent, jnp.float32) * width * loudness
    return jnp.minimum(jnp.maximum(drawn, -reach), reach).astype(held_as)


def setup_inputs(seed: int = 0) -> dict:
    keys = jax.random.split(jax.random.key(seed), 8)
    bag_grads = scatter_about(keys[0], (G * M * BAG_DEV, E), 1.0, 6.0, ((0, 768),), jnp.float32)
    bag_lengths = jax.vmap(lambda own: ragged_sizes(own, BAG_DEV, LOOK_DEV, 2 * POOL, 2))(jax.random.split(keys[1], (G * M))).reshape((G * M, BAG_DEV)).astype(jnp.int32)
    look_slot = draw_look_slot(jax.random.fold_in(keys[7], 71), 0)
    group_slot = draw_group_slot(jax.random.fold_in(keys[7], 71), 0)
    owner_row = draw_owner_row(jax.random.fold_in(keys[7], 71), 0)
    table = scatter_about(keys[5], (G * M * ROWS_DEV, E), 0.5, 3.0, ((0, 768),), jnp.float32)
    accum = jnp.clip(jnp.exp(math.log(4.0) - 2.0794415 * jax.random.uniform(keys[6], (G * M * ROWS_DEV,), jnp.float32) ** block_scale(keys[6], (G * M * ROWS_DEV,), ((0, 768),), -0.2, 0.2)), 0.5, 4.0)
    return {"bag_grads": bag_grads, "bag_lengths": bag_lengths, "look_slot": look_slot, "group_slot": group_slot, "owner_row": owner_row, "table": table, "accum": accum}


learn_rate = 0.3

def reference(bag_grads, bag_lengths, look_slot, group_slot, owner_row, table, accum):
    devices = G * M
    bag_ends = jnp.cumsum(bag_lengths, axis=1)
    places = jnp.arange(LOOK_DEV, dtype=jnp.int32)
    bag_of = lax.optimization_barrier(jnp.sum((places[None, :, None] >= bag_ends[:, None, :]).astype(jnp.int32), axis=2)).astype(jnp.int32)
    bag_table = bag_grads.reshape(devices, BAG_DEV, E)
    look_grads = jnp.take_along_axis(bag_table, bag_of[:, :, None], axis=1)
    device_ids = jnp.arange(devices, dtype=jnp.int32)[:, None]
    routed = jnp.zeros((devices, M * CAP1, E), jnp.float32).at[device_ids, look_slot].add(look_grads)
    arrived = routed.reshape(G, M, M, CAP1, E).transpose(0, 2, 1, 3, 4).reshape(devices, M * CAP1, E)
    group_map = group_slot.reshape(devices, M * CAP1)
    forwarded = jnp.zeros((devices, G * CAP2, E), jnp.float32).at[device_ids, group_map].add(arrived)
    landed = forwarded.reshape(G, M, G, CAP2, E).transpose(2, 1, 0, 3, 4).reshape(devices, G * CAP2, E)
    owner_rows = owner_row.reshape(devices, G * CAP2)

    def update(items):
        row_ids, grads_in, old_rows, old_accum = items
        row_grads = jnp.zeros((ROWS_DEV, E), jnp.float32).at[row_ids].add(grads_in)
        accum_next = old_accum + lax.optimization_barrier(jnp.mean(row_grads * row_grads, axis=1))
        rows_next = old_rows - learn_rate * row_grads / jnp.sqrt(accum_next)[:, None]
        return (rows_next, accum_next)
    new_table, new_accum = lax.map(update, (owner_rows, landed, table.reshape(devices, ROWS_DEV, E), accum.reshape(devices, ROWS_DEV)))
    serving = new_table.astype(jnp.bfloat16)
    picked = jnp.take_along_axis(serving, owner_rows[:, :, None], axis=1)
    returned = picked.reshape(G, M, G, CAP2, E).transpose(2, 1, 0, 3, 4).reshape(devices, G * CAP2, E)
    at_groups = jnp.take_along_axis(returned, group_map[:, :, None], axis=1)
    at_readers = at_groups.reshape(G, M, M, CAP1, E).transpose(0, 2, 1, 3, 4).reshape(devices, M * CAP1, E)
    fresh_rows = jnp.take_along_axis(at_readers, look_slot[:, :, None], axis=1)
    return (new_table.reshape(devices * ROWS_DEV, E), new_accum.reshape(devices * ROWS_DEV), fresh_rows.reshape(devices * LOOK_DEV, E))
```

```python
import functools

import jax
import jax.numpy as jnp
from jax import lax
from jax.experimental import pallas as pl
from jax.experimental.pallas import tpu as pltpu
from jax.sharding import PartitionSpec as P

learn_rate = 0.3
MESH = pl.DeviceIdType.MESH
GROUPS = 96
PLANES = 12
SIDES = 8
MEMBERS = 8
CAP1 = 24
PAD1 = 32
CAP2 = 2
ROWS = 1024
LOOKS = 512
BAGS = 32
WIDTH = 128
SLOTS = 192
F32 = jnp.float32
BF16 = jnp.bfloat16


def iota(shape, dim):
    return lax.broadcasted_iota(jnp.int32, shape, dim)


def hot(condition):
    return jnp.where(condition, 1.0, 0.0).astype(BF16)


def split3(value):
    high = value.astype(BF16)
    rest = value - high.astype(F32)
    middle = rest.astype(BF16)
    low = (rest - middle.astype(F32)).astype(BF16)
    return jnp.concatenate([high, middle, low], axis=1)


def mix(ones, value):
    parts = jnp.dot(ones, split3(value), preferred_element_type=F32)
    return parts[:, :WIDTH] + (parts[:, WIDTH : 2 * WIDTH] + parts[:, 2 * WIDTH :])


def kernel(
    grads_in,
    lengths_in,
    look_in,
    group_in,
    owner_in,
    table_in,
    accum_in,
    table_out,
    accum_out,
    fresh_out,
    grads,
    lengths,
    look,
    group,
    owner,
    table,
    accum,
    routed,
    arrived,
    forwarded,
    landed,
    picked,
    returned,
    back,
    reached,
    new_table,
    new_accum,
    fresh,
    load_sem,
    out_sem,
    own_sem,
    send_sem,
    recv_sem,
    plane_sem,
):
    o = lax.axis_index("outer")
    n = lax.axis_index("node")
    z = o // SIDES
    side = lax.rem(o, SIDES)
    loads = [
        pltpu.make_async_copy(source, target, load_sem.at[i])
        for i, (source, target) in enumerate(
            (
                (look_in, look),
                (lengths_in, lengths),
                (grads_in, grads),
                (group_in, group),
                (owner_in, owner),
                (accum_in, accum),
                (table_in, table),
            )
        )
    ]
    for load in loads:
        load.start()

    barrier = pltpu.get_barrier_semaphore()
    node_peers = [lax.rem(n + i, MEMBERS) for i in (4, 3, 5, 2, 6, 1, 7)]
    plane_peers = [lax.rem(z + i, PLANES) * SIDES + side for i in (6, 5, 7, 4, 8, 3, 9, 2, 10, 1, 11)]
    for p in node_peers:
        pl.semaphore_signal(barrier, 1, device_id={"node": p}, device_id_type=MESH)
    for p in plane_peers:
        pl.semaphore_signal(barrier, 1, device_id={"outer": p}, device_id_type=MESH)
    for i in range(1, SIDES):
        p = z * SIDES + lax.rem(side + i, SIDES)
        pl.semaphore_signal(barrier, 1, device_id={"outer": p}, device_id_type=MESH)

    loads[0].wait()
    loads[1].wait()
    loads[2].wait()
    before = jnp.where(iota((BAGS, BAGS), 1) <= iota((BAGS, BAGS), 0), lengths[...], 0)
    ends = jnp.sum(before, axis=1, keepdims=True)
    own = jnp.where(iota((BAGS, BAGS), 1) == iota((BAGS, BAGS), 0), lengths[...], 0)
    starts = ends - jnp.sum(own, axis=1, keepdims=True)
    place = iota((BAGS, LOOKS), 1)
    of_bag = hot((place >= starts) & (place < ends))
    of_slot = hot(iota((SLOTS, LOOKS), 0) == look[...])
    counts = lax.dot_general(of_slot, of_bag, (((1,), (1,)), ((), ())), preferred_element_type=F32)
    routed[...] = mix(counts.astype(BF16), grads[...]).reshape(MEMBERS, CAP1, WIDTH)

    pl.semaphore_wait(barrier, MEMBERS - 1 + PLANES - 1 + SIDES - 1)
    for p in node_peers:
        pltpu.make_async_remote_copy(
            routed.at[p], arrived.at[n], send_sem.at[0], recv_sem.at[0], device_id={"node": p}, device_id_type=MESH
        ).start()
    for p in plane_peers:
        pl.semaphore_signal(plane_sem, 1, device_id={"outer": p}, device_id_type=MESH)
    arrived[n] = routed[n]

    loads[3].wait()
    sender = lax.shift_right_logical(iota((MEMBERS, SLOTS), 1) * 2731, 16)
    column = lax.shift_right_logical(iota((CAP1, SLOTS), 1) * 2731, 16)
    spread = hot(iota((CAP1, SLOTS), 1) - CAP1 * column == iota((CAP1, SLOTS), 0))
    slots = jnp.dot(group[0].astype(F32).astype(BF16), spread, preferred_element_type=F32)
    group_row = jnp.sum(jnp.where(sender == iota((MEMBERS, SLOTS), 0), slots, 0.0), axis=0, keepdims=True).astype(jnp.int32)
    to_group = hot(iota((SLOTS, SLOTS), 0) == group_row)

    landing = arrived.at[pl.ds(0, MEMBERS - 1)]
    pltpu.make_async_copy(landing, landing, recv_sem.at[0]).wait()
    forwarded[...] = mix(to_group, arrived[...].reshape(SLOTS, WIDTH))
    pl.semaphore_wait(plane_sem, PLANES - 1)

    def outer_peer(i):
        return lax.rem(o + i, GROUPS)

    def exchange(source, target, index):
        def send(i, carry):
            p = outer_peer(i)
            pltpu.make_async_remote_copy(
                source.at[pl.ds(CAP2 * p, CAP2)],
                target.at[pl.ds(CAP2 * o, CAP2)],
                send_sem.at[index],
                recv_sem.at[index],
                device_id={"outer": p},
                device_id_type=MESH,
            ).start()
            return carry

        lax.fori_loop(1, GROUPS, send, 0, unroll=5)
        mine = pltpu.make_async_copy(
            source.at[pl.ds(CAP2 * o, CAP2)], target.at[pl.ds(CAP2 * o, CAP2)], own_sem.at[index - 1]
        )
        mine.start()
        return mine

    def rows_of(ref, rows):
        return ref.at[pl.ds(0, rows)]

    def wait_bytes(part, semaphore):
        pltpu.make_async_copy(part, part, semaphore).wait()

    mine_forward = exchange(forwarded, landed, 1)

    loads[4].wait()
    loads[5].wait()
    loads[6].wait()
    owner_high = lax.shift_right_logical(owner[0], 5)
    owner_low = owner[0] - 32 * owner_high
    digits = jnp.concatenate([owner_high, owner_low], axis=0).astype(F32).astype(BF16)
    pair = hot(lax.shift_right_logical(iota((GROUPS, SLOTS), 1), 1) == iota((GROUPS, SLOTS), 0))
    laid = jnp.dot(digits, pair, preferred_element_type=F32)
    even = (iota((1, SLOTS), 1) & 1) == 0
    owner_row = 32.0 * jnp.where(even, laid[0:1], laid[1:2]) + jnp.where(even, laid[2:3], laid[3:4])
    owner_row = owner_row.astype(jnp.int32)
    diagonal = iota((SLOTS, SLOTS), 0) == iota((SLOTS, SLOTS), 1)
    owner_column = jnp.sum(jnp.where(diagonal, owner_row, 0), axis=1, keepdims=True)
    same_row = hot(owner_column == owner_row)
    to_row = hot(iota((ROWS, SLOTS), 0) == owner_row)
    from_row = hot(owner_column == iota((SLOTS, ROWS), 1))
    old_rows = mix(from_row, table[...])
    by_lane = jnp.where((owner_column & 127) == iota((SLOTS, WIDTH), 1), 1.0, 0.0)
    by_block = lax.shift_right_logical(owner_column, 7)
    chosen = jnp.zeros((SLOTS, WIDTH), F32)
    for a in range(ROWS // WIDTH):
        chosen = jnp.where(by_block == a, accum[a : a + 1, :], chosen)
    old_accum = jnp.sum(chosen * by_lane, axis=1, keepdims=True)

    padded = iota((MEMBERS * PAD1, SLOTS), 0)
    slot_place = iota((MEMBERS * PAD1, SLOTS), 1)
    spaced = hot(slot_place + 8 * lax.shift_right_logical(slot_place * 2731, 16) == padded)
    from_group = lax.dot_general(spaced, to_group, (((1,), (1,)), ((), ())), preferred_element_type=F32).astype(BF16)
    look_spaced = look[...] + 8 * lax.shift_right_logical(look[...] * 2731, 16)
    look_hot = hot(iota((MEMBERS * PAD1, LOOKS), 0) == look_spaced)
    eye = hot(iota((LOOKS, LOOKS), 0) == iota((LOOKS, LOOKS), 1))
    from_look = lax.dot_general(eye, look_hot, (((1,), (1,)), ((), ())), preferred_element_type=F32).astype(BF16)

    mine_forward.wait()
    wait_bytes(rows_of(landed, SLOTS - CAP2), recv_sem.at[1])
    came = split3(landed[...])
    sums = jnp.dot(same_row, came, preferred_element_type=F32)
    slot_grads = sums[:, :WIDTH] + (sums[:, WIDTH : 2 * WIDTH] + sums[:, 2 * WIDTH :])
    slot_accum = old_accum + jnp.mean(slot_grads * slot_grads, axis=1, keepdims=True)
    fresh_slots = old_rows - learn_rate * slot_grads / jnp.sqrt(slot_accum)
    picked[...] = fresh_slots.astype(BF16).astype(F32)
    mine_picked = exchange(picked, returned, 2)

    turned = jnp.transpose(jnp.concatenate([accum[...]] * (WIDTH // 8), axis=0))
    next_accum = jnp.zeros((WIDTH, WIDTH), F32)
    lane = iota((WIDTH, WIDTH), 1)
    for a in range(ROWS // WIDTH):
        part = slice(a * WIDTH, (a + 1) * WIDTH)
        sums = jnp.dot(to_row[part], came, preferred_element_type=F32)
        row_grads = sums[:, :WIDTH] + (sums[:, WIDTH : 2 * WIDTH] + sums[:, 2 * WIDTH :])
        row_accum = turned[:, a : a + 1] + jnp.mean(row_grads * row_grads, axis=1, keepdims=True)
        new_table[part, :] = table[part, :] - learn_rate * row_grads / jnp.sqrt(row_accum)
        next_accum = jnp.where(lane == a, row_accum, next_accum)
    new_accum[...] = jnp.transpose(next_accum)[: ROWS // WIDTH]
    table_copy = pltpu.make_async_copy(new_table, table_out, out_sem.at[0])
    table_copy.start()
    accum_copy = pltpu.make_async_copy(new_accum, accum_out, out_sem.at[1])
    accum_copy.start()

    mine_picked.wait()
    wait_bytes(rows_of(returned, SLOTS - CAP2), recv_sem.at[2])
    gathered = jnp.dot(from_group, returned[...].astype(BF16), preferred_element_type=F32)
    back[...] = gathered.astype(BF16).reshape(MEMBERS, PAD1, WIDTH)
    for p in node_peers:
        pltpu.make_async_remote_copy(
            back.at[p], reached.at[n], send_sem.at[3], recv_sem.at[3], device_id={"node": p}, device_id_type=MESH
        ).start()
    reached[n] = back[n]

    landing = reached.at[pl.ds(0, MEMBERS - 1)]
    wait_bytes(landing, recv_sem.at[3])
    read = jnp.dot(from_look, reached[...].reshape(MEMBERS * PAD1, WIDTH), preferred_element_type=F32)
    fresh[...] = read.astype(BF16)
    fresh_copy = pltpu.make_async_copy(fresh, fresh_out, out_sem.at[2])
    fresh_copy.start()

    wait_bytes(routed.at[pl.ds(0, MEMBERS - 1)], send_sem.at[0])
    wait_bytes(rows_of(forwarded, SLOTS - CAP2), send_sem.at[1])
    wait_bytes(rows_of(picked, SLOTS - CAP2), send_sem.at[2])
    wait_bytes(back.at[pl.ds(0, MEMBERS - 1)], send_sem.at[3])
    table_copy.wait()
    accum_copy.wait()
    fresh_copy.wait()


def on_device(bag_grads, bag_lengths, look_slot, group_slot, owner_row, table, accum):
    outs = pl.pallas_call(
        kernel,
        out_shape=(
            jax.ShapeDtypeStruct((ROWS, WIDTH), F32),
            jax.ShapeDtypeStruct((ROWS // WIDTH, WIDTH), F32),
            jax.ShapeDtypeStruct((LOOKS, WIDTH), BF16),
        ),
        in_specs=[pl.BlockSpec(memory_space=pltpu.HBM)] * 7,
        out_specs=[pl.BlockSpec(memory_space=pltpu.HBM)] * 3,
        scratch_shapes=[
            pltpu.VMEM((BAGS, WIDTH), F32),
            pltpu.VMEM((1, BAGS), jnp.int32),
            pltpu.VMEM((1, LOOKS), jnp.int32),
            pltpu.VMEM((1, MEMBERS, CAP1), jnp.int32),
            pltpu.VMEM((1, CAP2, GROUPS), jnp.int32),
            pltpu.VMEM((ROWS, WIDTH), F32),
            pltpu.VMEM((ROWS // WIDTH, WIDTH), F32),
            pltpu.VMEM((MEMBERS, CAP1, WIDTH), F32),
            pltpu.VMEM((MEMBERS, CAP1, WIDTH), F32),
            pltpu.VMEM((SLOTS, WIDTH), F32),
            pltpu.VMEM((SLOTS, WIDTH), F32),
            pltpu.VMEM((SLOTS, WIDTH), F32),
            pltpu.VMEM((SLOTS, WIDTH), F32),
            pltpu.VMEM((MEMBERS, PAD1, WIDTH), BF16),
            pltpu.VMEM((MEMBERS, PAD1, WIDTH), BF16),
            pltpu.VMEM((ROWS, WIDTH), F32),
            pltpu.VMEM((ROWS // WIDTH, WIDTH), F32),
            pltpu.VMEM((LOOKS, WIDTH), BF16),
            pltpu.SemaphoreType.DMA((7,)),
            pltpu.SemaphoreType.DMA((3,)),
            pltpu.SemaphoreType.DMA((2,)),
            pltpu.SemaphoreType.DMA((4,)),
            pltpu.SemaphoreType.DMA((4,)),
            pltpu.SemaphoreType.REGULAR,
        ],
        compiler_params=pltpu.CompilerParams(collective_id=0, has_side_effects=True, vmem_limit_bytes=32 * 1024 * 1024),
        cost_estimate=pl.CostEstimate(flops=600_000_000, bytes_accessed=1_400_000, transcendentals=1024),
    )(
        bag_grads,
        bag_lengths,
        look_slot,
        group_slot,
        jnp.transpose(owner_row, (0, 2, 1)),
        table,
        accum.reshape(ROWS // WIDTH, WIDTH),
    )
    return outs[0], outs[1].reshape(ROWS), outs[2]


def solution(mesh):
    both = ("outer", "node")
    placed = (
        P(both, None),
        P(both, None),
        P(both, None),
        P(both, None, None),
        P(both, None, None),
        P(both, None),
        P(both),
    )
    return jax.shard_map(
        on_device,
        mesh=mesh,
        in_specs=placed,
        out_specs=(P(both, None), P(both), P(both, None)),
        check_vma=False,
    )
```

```python
import functools

import jax
import jax.numpy as jnp
from jax import lax
from jax.experimental import pallas as pl
from jax.experimental.pallas import tpu as pltpu
from jax.sharding import PartitionSpec as P

learn_rate = 0.3
MESH = pl.DeviceIdType.MESH
GROUPS = 96
FAR_FIRST = (6, 5, 7, 4, 8, 3, 9, 2, 10, 1, 11, 0)
PLANES = 12
SIDES = 8
MEMBERS = 8
CAP1 = 24
PAD1 = 32
CAP2 = 2
ROWS = 1024
LOOKS = 512
BAGS = 32
WIDTH = 128
SLOTS = 192
F32 = jnp.float32
BF16 = jnp.bfloat16


def iota(shape, dim):
    return lax.broadcasted_iota(jnp.int32, shape, dim)


def hot(condition):
    return jnp.where(condition, 1.0, 0.0).astype(BF16)


def split3(value):
    high = value.astype(BF16)
    rest = value - high.astype(F32)
    middle = rest.astype(BF16)
    low = (rest - middle.astype(F32)).astype(BF16)
    return jnp.concatenate([high, middle, low], axis=1)


def mix(ones, value):
    parts = jnp.dot(ones, split3(value), preferred_element_type=F32)
    return parts[:, :WIDTH] + (parts[:, WIDTH : 2 * WIDTH] + parts[:, 2 * WIDTH :])


def kernel(
    grads_in,
    lengths_in,
    look_in,
    group_in,
    owner_in,
    table_in,
    accum_in,
    new_table,
    new_accum,
    fresh,
    grads,
    lengths,
    look,
    group,
    owner,
    table,
    accum,
    routed,
    arrived,
    forwarded,
    landed,
    picked,
    returned,
    back,
    reached,
    load_sem,
    own_sem,
    send_sem,
    recv_sem,
    plane_sem,
):
    o = lax.axis_index("outer")
    n = lax.axis_index("node")
    z = o // SIDES
    side = lax.rem(o, SIDES)
    loads = [
        pltpu.make_async_copy(source, target, load_sem.at[i])
        for i, (source, target) in enumerate(
            (
                (look_in, look),
                (lengths_in, lengths),
                (grads_in, grads),
                (group_in, group),
                (owner_in, owner),
                (accum_in, accum),
                (table_in, table),
            )
        )
    ]
    for load in loads:
        load.start()

    barrier = pltpu.get_barrier_semaphore()
    node_peers = [lax.rem(n + i, MEMBERS) for i in (4, 3, 5, 2, 6, 1, 7)]
    plane_peers = [lax.rem(z + i, PLANES) * SIDES + side for i in (6, 5, 7, 4, 8, 3, 9, 2, 10, 1, 11)]
    for p in node_peers:
        pl.semaphore_signal(barrier, 1, device_id={"node": p}, device_id_type=MESH)
    for p in plane_peers:
        pl.semaphore_signal(barrier, 1, device_id={"outer": p}, device_id_type=MESH)
    for i in range(1, SIDES):
        p = z * SIDES + lax.rem(side + i, SIDES)
        pl.semaphore_signal(barrier, 1, device_id={"outer": p}, device_id_type=MESH)

    loads[0].wait()
    loads[1].wait()
    loads[2].wait()
    before = jnp.where(iota((BAGS, BAGS), 1) <= iota((BAGS, BAGS), 0), lengths[...], 0)
    ends = jnp.sum(before, axis=1, keepdims=True)
    own = jnp.where(iota((BAGS, BAGS), 1) == iota((BAGS, BAGS), 0), lengths[...], 0)
    starts = ends - jnp.sum(own, axis=1, keepdims=True)
    place = iota((BAGS, LOOKS), 1)
    of_bag = hot((place >= starts) & (place < ends))
    of_slot = hot(iota((SLOTS, LOOKS), 0) == look[...])
    counts = lax.dot_general(of_slot, of_bag, (((1,), (1,)), ((), ())), preferred_element_type=F32)
    routed[...] = mix(counts.astype(BF16), grads[...]).reshape(MEMBERS, CAP1, WIDTH)

    pl.semaphore_wait(barrier, MEMBERS - 1 + PLANES - 1 + SIDES - 1)
    for p in node_peers:
        pltpu.make_async_remote_copy(
            routed.at[p], arrived.at[n], send_sem.at[0], recv_sem.at[0], device_id={"node": p}, device_id_type=MESH
        ).start()
    for p in plane_peers:
        pl.semaphore_signal(plane_sem, 1, device_id={"outer": p}, device_id_type=MESH)
    arrived[n] = routed[n]

    loads[3].wait()
    sender = lax.shift_right_logical(iota((MEMBERS, SLOTS), 1) * 2731, 16)
    column = lax.shift_right_logical(iota((CAP1, SLOTS), 1) * 2731, 16)
    spread = hot(iota((CAP1, SLOTS), 1) - CAP1 * column == iota((CAP1, SLOTS), 0))
    slots = jnp.dot(group[0].astype(F32).astype(BF16), spread, preferred_element_type=F32)
    group_row = jnp.sum(jnp.where(sender == iota((MEMBERS, SLOTS), 0), slots, 0.0), axis=0, keepdims=True).astype(jnp.int32)
    to_group = hot(iota((SLOTS, SLOTS), 0) == group_row)

    landing = arrived.at[pl.ds(0, MEMBERS - 1)]
    pltpu.make_async_copy(landing, landing, recv_sem.at[0]).wait()
    forwarded[...] = mix(to_group, arrived[...].reshape(SLOTS, WIDTH))
    pl.semaphore_wait(plane_sem, PLANES - 1)

    def exchange(source, target, index, order):
        for away in order:
            plane = lax.rem(z + away, PLANES) * SIDES

            def send(i, carry, plane=plane):
                p = plane + lax.rem(side + i, SIDES)
                pltpu.make_async_remote_copy(
                    source.at[pl.ds(CAP2 * p, CAP2)],
                    target.at[pl.ds(CAP2 * o, CAP2)],
                    send_sem.at[index],
                    recv_sem.at[index],
                    device_id={"outer": p},
                    device_id_type=MESH,
                ).start()
                return carry

            lax.fori_loop(1 if away == 0 else 0, SIDES, send, 0, unroll=7 if away == 0 else 8)
        mine = pltpu.make_async_copy(
            source.at[pl.ds(CAP2 * o, CAP2)], target.at[pl.ds(CAP2 * o, CAP2)], own_sem.at[index - 1]
        )
        mine.start()
        return mine

    def rows_of(ref, rows):
        return ref.at[pl.ds(0, rows)]

    def wait_bytes(part, semaphore):
        pltpu.make_async_copy(part, part, semaphore).wait()

    mine_forward = exchange(forwarded, landed, 1, FAR_FIRST)

    loads[4].wait()
    loads[5].wait()
    loads[6].wait()
    owner_high = lax.shift_right_logical(owner[0], 5)
    owner_low = owner[0] - 32 * owner_high
    digits = jnp.concatenate([owner_high, owner_low], axis=0).astype(F32).astype(BF16)
    pair = hot(lax.shift_right_logical(iota((GROUPS, SLOTS), 1), 1) == iota((GROUPS, SLOTS), 0))
    laid = jnp.dot(digits, pair, preferred_element_type=F32)
    even = (iota((1, SLOTS), 1) & 1) == 0
    owner_row = 32.0 * jnp.where(even, laid[0:1], laid[1:2]) + jnp.where(even, laid[2:3], laid[3:4])
    owner_row = owner_row.astype(jnp.int32)
    diagonal = iota((SLOTS, SLOTS), 0) == iota((SLOTS, SLOTS), 1)
    owner_column = jnp.sum(jnp.where(diagonal, owner_row, 0), axis=1, keepdims=True)
    same_row = hot(owner_column == owner_row)
    to_row = hot(iota((ROWS, SLOTS), 0) == owner_row)
    from_row = hot(owner_column == iota((SLOTS, ROWS), 1))
    old_rows = mix(from_row, table[...])
    by_lane = jnp.where((owner_column & 127) == iota((SLOTS, WIDTH), 1), 1.0, 0.0)
    by_block = lax.shift_right_logical(owner_column, 7)
    chosen = jnp.zeros((SLOTS, WIDTH), F32)
    for a in range(ROWS // WIDTH):
        chosen = jnp.where(by_block == a, accum[a : a + 1, :], chosen)
    old_accum = jnp.sum(chosen * by_lane, axis=1, keepdims=True)

    padded = iota((MEMBERS * PAD1, SLOTS), 0)
    slot_place = iota((MEMBERS * PAD1, SLOTS), 1)
    spaced = hot(slot_place + 8 * lax.shift_right_logical(slot_place * 2731, 16) == padded)
    from_group = lax.dot_general(spaced, to_group, (((1,), (1,)), ((), ())), preferred_element_type=F32).astype(BF16)
    look_spaced = look[...] + 8 * lax.shift_right_logical(look[...] * 2731, 16)
    look_hot = hot(iota((MEMBERS * PAD1, LOOKS), 0) == look_spaced)
    eye = hot(iota((LOOKS, LOOKS), 0) == iota((LOOKS, LOOKS), 1))
    from_look = lax.dot_general(eye, look_hot, (((1,), (1,)), ((), ())), preferred_element_type=F32).astype(BF16)

    mine_forward.wait()
    wait_bytes(rows_of(landed, SLOTS - CAP2), recv_sem.at[1])
    came = split3(landed[...])
    sums = jnp.dot(same_row, came, preferred_element_type=F32)
    slot_grads = sums[:, :WIDTH] + (sums[:, WIDTH : 2 * WIDTH] + sums[:, 2 * WIDTH :])
    slot_accum = old_accum + jnp.mean(slot_grads * slot_grads, axis=1, keepdims=True)
    fresh_slots = old_rows - learn_rate * slot_grads / jnp.sqrt(slot_accum)
    picked[...] = fresh_slots.astype(BF16).astype(F32)
    mine_picked = exchange(picked, returned, 2, FAR_FIRST)

    turned = jnp.transpose(jnp.concatenate([accum[...]] * (WIDTH // 8), axis=0))
    next_accum = jnp.zeros((WIDTH, WIDTH), F32)
    lane = iota((WIDTH, WIDTH), 1)
    for a in range(ROWS // WIDTH):
        part = slice(a * WIDTH, (a + 1) * WIDTH)
        sums = jnp.dot(to_row[part], came, preferred_element_type=F32)
        row_grads = sums[:, :WIDTH] + (sums[:, WIDTH : 2 * WIDTH] + sums[:, 2 * WIDTH :])
        row_accum = turned[:, a : a + 1] + jnp.mean(row_grads * row_grads, axis=1, keepdims=True)
        new_table[part, :] = table[part, :] - learn_rate * row_grads / jnp.sqrt(row_accum)
        next_accum = jnp.where(lane == a, row_accum, next_accum)
    new_accum[...] = jnp.transpose(next_accum)[: ROWS // WIDTH]

    mine_picked.wait()
    wait_bytes(rows_of(returned, SLOTS - CAP2), recv_sem.at[2])
    gathered = jnp.dot(from_group, returned[...].astype(BF16), preferred_element_type=F32)
    back[...] = gathered.astype(BF16).reshape(MEMBERS, PAD1, WIDTH)
    for p in node_peers:
        pltpu.make_async_remote_copy(
            back.at[p], reached.at[n], send_sem.at[3], recv_sem.at[3], device_id={"node": p}, device_id_type=MESH
        ).start()
    reached[n] = back[n]

    landing = reached.at[pl.ds(0, MEMBERS - 1)]
    wait_bytes(landing, recv_sem.at[3])
    read = jnp.dot(from_look, reached[...].reshape(MEMBERS * PAD1, WIDTH), preferred_element_type=F32)
    fresh[...] = read.astype(BF16)

    wait_bytes(routed.at[pl.ds(0, MEMBERS - 1)], send_sem.at[0])
    wait_bytes(rows_of(forwarded, SLOTS - CAP2), send_sem.at[1])
    wait_bytes(rows_of(picked, SLOTS - CAP2), send_sem.at[2])
    wait_bytes(back.at[pl.ds(0, MEMBERS - 1)], send_sem.at[3])


def hand_over(table, accum, fresh, table_out, accum_out, fresh_out, sem):
    copies = [
        pltpu.make_async_copy(source, target, sem.at[i])
        for i, (source, target) in enumerate(((table, table_out), (fresh, fresh_out), (accum, accum_out)))
    ]
    for copy in copies:
        copy.start()
    for copy in copies:
        copy.wait()


def on_device(bag_grads, bag_lengths, look_slot, group_slot, owner_row, table, accum):
    outs = pl.pallas_call(
        kernel,
        out_shape=(
            jax.ShapeDtypeStruct((ROWS, WIDTH), F32),
            jax.ShapeDtypeStruct((ROWS // WIDTH, WIDTH), F32),
            jax.ShapeDtypeStruct((LOOKS, WIDTH), BF16),
        ),
        in_specs=[pl.BlockSpec(memory_space=pltpu.HBM)] * 7,
        out_specs=[pl.BlockSpec(memory_space=pltpu.VMEM)] * 3,
        scratch_shapes=[
            pltpu.VMEM((BAGS, WIDTH), F32),
            pltpu.VMEM((1, BAGS), jnp.int32),
            pltpu.VMEM((1, LOOKS), jnp.int32),
            pltpu.VMEM((1, MEMBERS, CAP1), jnp.int32),
            pltpu.VMEM((1, CAP2, GROUPS), jnp.int32),
            pltpu.VMEM((ROWS, WIDTH), F32),
            pltpu.VMEM((ROWS // WIDTH, WIDTH), F32),
            pltpu.VMEM((MEMBERS, CAP1, WIDTH), F32),
            pltpu.VMEM((MEMBERS, CAP1, WIDTH), F32),
            pltpu.VMEM((SLOTS, WIDTH), F32),
            pltpu.VMEM((SLOTS, WIDTH), F32),
            pltpu.VMEM((SLOTS, WIDTH), F32),
            pltpu.VMEM((SLOTS, WIDTH), F32),
            pltpu.VMEM((MEMBERS, PAD1, WIDTH), BF16),
            pltpu.VMEM((MEMBERS, PAD1, WIDTH), BF16),
            pltpu.SemaphoreType.DMA((7,)),
            pltpu.SemaphoreType.DMA((2,)),
            pltpu.SemaphoreType.DMA((4,)),
            pltpu.SemaphoreType.DMA((4,)),
            pltpu.SemaphoreType.REGULAR,
        ],
        compiler_params=pltpu.CompilerParams(collective_id=0, has_side_effects=True, vmem_limit_bytes=32 * 1024 * 1024),
        cost_estimate=pl.CostEstimate(flops=600_000_000, bytes_accessed=1_400_000, transcendentals=1024),
    )(
        *[pltpu.with_memory_space_constraint(a, pltpu.HBM) for a in (bag_grads, bag_lengths, look_slot, group_slot, jnp.transpose(owner_row, (0, 2, 1)), table, accum.reshape(ROWS // WIDTH, WIDTH))]
    )
    table, accum, fresh = pl.pallas_call(
        hand_over,
        out_shape=[jax.ShapeDtypeStruct(out.shape, out.dtype) for out in outs],
        in_specs=[pl.BlockSpec(memory_space=pltpu.VMEM)] * 3,
        out_specs=[pl.BlockSpec(memory_space=pltpu.HBM)] * 3,
        scratch_shapes=[pltpu.SemaphoreType.DMA((3,))],
        compiler_params=pltpu.CompilerParams(vmem_limit_bytes=16 * 1024 * 1024),
        cost_estimate=pl.CostEstimate(flops=0, bytes_accessed=1_400_000, transcendentals=0),
    )(*outs)
    return table, accum.reshape(ROWS), fresh


def solution(mesh):
    both = ("outer", "node")
    placed = (
        P(both, None),
        P(both, None),
        P(both, None),
        P(both, None, None),
        P(both, None, None),
        P(both, None),
        P(both),
    )
    return jax.shard_map(
        on_device,
        mesh=mesh,
        in_specs=placed,
        out_specs=(P(both, None), P(both), P(both, None)),
        check_vma=False,
    )
```

```python
import functools

import jax
import jax.numpy as jnp
from jax import lax
from jax.experimental import pallas as pl
from jax.experimental.pallas import tpu as pltpu
from jax.sharding import PartitionSpec as P

learn_rate = 0.3
MESH = pl.DeviceIdType.MESH
GROUPS = 96
FROM_FAR = (6, 5, 7, 4, 8, 3, 9, 2, 10, 1, 11, 0)
FROM_NEAR = (0, 1, 2, 3, 4, 5, 6, 7, 8, 9, 10, 11)
PLANES = 12
SIDES = 8
MEMBERS = 8
CAP1 = 24
PAD1 = 32
CAP2 = 2
ROWS = 1024
LOOKS = 512
BAGS = 32
WIDTH = 128
SLOTS = 192
F32 = jnp.float32
BF16 = jnp.bfloat16


def iota(shape, dim):
    return lax.broadcasted_iota(jnp.int32, shape, dim)


def hot(condition):
    return jnp.where(condition, 1.0, 0.0).astype(BF16)


def split3(value):
    high = value.astype(BF16)
    rest = value - high.astype(F32)
    middle = rest.astype(BF16)
    low = (rest - middle.astype(F32)).astype(BF16)
    return jnp.concatenate([high, middle, low], axis=1)


def mix(ones, value):
    parts = jnp.dot(ones, split3(value), preferred_element_type=F32)
    return parts[:, :WIDTH] + (parts[:, WIDTH : 2 * WIDTH] + parts[:, 2 * WIDTH :])


def kernel(
    grads_in,
    lengths_in,
    look_in,
    group_in,
    owner_in,
    table_in,
    accum_in,
    new_table,
    new_accum,
    from_look,
    reached,
    grads,
    lengths,
    look,
    group,
    owner,
    table,
    accum,
    routed,
    arrived,
    forwarded,
    landed,
    picked,
    returned,
    back,
    load_sem,
    own_sem,
    send_sem,
    recv_sem,
    side_sem,
):
    o = lax.axis_index("outer")
    n = lax.axis_index("node")
    z = o // SIDES
    side = lax.rem(o, SIDES)
    loads = [
        pltpu.make_async_copy(source, target, load_sem.at[i])
        for i, (source, target) in enumerate(
            (
                (look_in, look),
                (lengths_in, lengths),
                (grads_in, grads),
                (group_in, group),
                (owner_in, owner),
                (accum_in, accum),
                (table_in, table),
            )
        )
    ]
    for load in loads:
        load.start()

    barrier = pltpu.get_barrier_semaphore()
    node_peers = [lax.rem(n + i, MEMBERS) for i in (4, 3, 5, 2, 6, 1, 7)]
    plane_peers = [lax.rem(z + i, PLANES) * SIDES + side for i in (6, 5, 7, 4, 8, 3, 9, 2, 10, 1, 11)]
    side_peers = [z * SIDES + lax.rem(side + i, SIDES) for i in (4, 3, 5, 2, 6, 1, 7)]
    for p in node_peers:
        pl.semaphore_signal(barrier, 1, device_id={"node": p}, device_id_type=MESH)
    for p in plane_peers:
        pl.semaphore_signal(barrier, 1, device_id={"outer": p}, device_id_type=MESH)
    for p in side_peers:
        pl.semaphore_signal(barrier, 1, device_id={"outer": p}, device_id_type=MESH)

    loads[0].wait()
    loads[1].wait()
    loads[2].wait()
    before = jnp.where(iota((BAGS, BAGS), 1) <= iota((BAGS, BAGS), 0), lengths[...], 0)
    ends = jnp.sum(before, axis=1, keepdims=True)
    own = jnp.where(iota((BAGS, BAGS), 1) == iota((BAGS, BAGS), 0), lengths[...], 0)
    starts = ends - jnp.sum(own, axis=1, keepdims=True)
    place = iota((BAGS, LOOKS), 1)
    of_bag = hot((place >= starts) & (place < ends))
    of_slot = hot(iota((SLOTS, LOOKS), 0) == look[...])
    counts = lax.dot_general(of_slot, of_bag, (((1,), (1,)), ((), ())), preferred_element_type=F32)
    routed[...] = mix(counts.astype(BF16), grads[...]).reshape(MEMBERS, CAP1, WIDTH)

    pl.semaphore_wait(barrier, MEMBERS - 1 + PLANES - 1 + SIDES - 1)
    for p in node_peers:
        pltpu.make_async_remote_copy(
            routed.at[p], arrived.at[n], send_sem.at[0], recv_sem.at[0], device_id={"node": p}, device_id_type=MESH
        ).start()
    for p in side_peers:
        pl.semaphore_signal(side_sem, 1, device_id={"outer": p}, device_id_type=MESH)
    arrived[n] = routed[n]

    loads[3].wait()
    sender = lax.shift_right_logical(iota((MEMBERS, SLOTS), 1) * 2731, 16)
    column = lax.shift_right_logical(iota((CAP1, SLOTS), 1) * 2731, 16)
    spread = hot(iota((CAP1, SLOTS), 1) - CAP1 * column == iota((CAP1, SLOTS), 0))
    slots = jnp.dot(group[0].astype(F32).astype(BF16), spread, preferred_element_type=F32)
    group_row = jnp.sum(jnp.where(sender == iota((MEMBERS, SLOTS), 0), slots, 0.0), axis=0, keepdims=True).astype(jnp.int32)
    to_group = hot(iota((SLOTS, SLOTS), 0) == group_row)

    landing = arrived.at[pl.ds(0, MEMBERS - 1)]
    pltpu.make_async_copy(landing, landing, recv_sem.at[0]).wait()
    forwarded[...] = mix(to_group, arrived[...].reshape(SLOTS, WIDTH))
    pl.semaphore_wait(side_sem, SIDES - 1)

    def block(ref, group):
        return ref.at[pl.ds(CAP2 * group, CAP2)] if len(ref.shape) == 2 else ref.at[group]

    def exchange(source, target, index, order):
        for place_z in order:
            plane = place_z * SIDES

            def send(i, carry, plane=plane):
                p = plane + lax.rem(side + i, SIDES)
                pltpu.make_async_remote_copy(
                    block(source, p),
                    block(target, o),
                    send_sem.at[index],
                    recv_sem.at[index],
                    device_id={"outer": p},
                    device_id_type=MESH,
                ).start()
                return carry

            lax.fori_loop(1, SIDES, send, 0, unroll=7)

            @pl.when(z != place_z)
            def _(plane=plane, send=send):
                send(0, 0)
        mine = pltpu.make_async_copy(
            block(source, o), block(target, o), own_sem.at[index - 1]
        )
        mine.start()
        return mine

    def rows_of(ref, rows):
        return ref.at[pl.ds(0, rows)]

    def wait_bytes(part, semaphore):
        pltpu.make_async_copy(part, part, semaphore).wait()

    mine_forward = exchange(forwarded, landed, 1, FROM_FAR)

    loads[4].wait()
    loads[5].wait()
    loads[6].wait()
    owner_high = lax.shift_right_logical(owner[0], 5)
    owner_low = owner[0] - 32 * owner_high
    digits = jnp.concatenate([owner_high, owner_low], axis=0).astype(F32).astype(BF16)
    pair = hot(lax.shift_right_logical(iota((GROUPS, SLOTS), 1), 1) == iota((GROUPS, SLOTS), 0))
    laid = jnp.dot(digits, pair, preferred_element_type=F32)
    even = (iota((1, SLOTS), 1) & 1) == 0
    owner_row = 32.0 * jnp.where(even, laid[0:1], laid[1:2]) + jnp.where(even, laid[2:3], laid[3:4])
    owner_row = owner_row.astype(jnp.int32)
    diagonal = iota((SLOTS, SLOTS), 0) == iota((SLOTS, SLOTS), 1)
    owner_column = jnp.sum(jnp.where(diagonal, owner_row, 0), axis=1, keepdims=True)
    same_row = hot(owner_column == owner_row)
    to_row = hot(iota((ROWS, SLOTS), 0) == owner_row)
    from_row = hot(owner_column == iota((SLOTS, ROWS), 1))
    old_rows = mix(from_row, table[...])
    by_lane = jnp.where((owner_column & 127) == iota((SLOTS, WIDTH), 1), 1.0, 0.0)
    by_block = lax.shift_right_logical(owner_column, 7)
    chosen = jnp.zeros((SLOTS, WIDTH), F32)
    for a in range(ROWS // WIDTH):
        chosen = jnp.where(by_block == a, accum[a : a + 1, :], chosen)
    old_accum = jnp.sum(chosen * by_lane, axis=1, keepdims=True)

    padded = iota((MEMBERS * PAD1, SLOTS), 0)
    slot_place = iota((MEMBERS * PAD1, SLOTS), 1)
    spaced = hot(slot_place + 8 * lax.shift_right_logical(slot_place * 2731, 16) == padded)
    from_group = lax.dot_general(spaced, to_group, (((1,), (1,)), ((), ())), preferred_element_type=F32).astype(BF16)
    look_spaced = look[...] + 8 * lax.shift_right_logical(look[...] * 2731, 16)
    look_hot = hot(iota((MEMBERS * PAD1, LOOKS), 0) == look_spaced)
    eye = hot(iota((LOOKS, LOOKS), 0) == iota((LOOKS, LOOKS), 1))
    turned_look = lax.dot_general(eye, look_hot, (((1,), (1,)), ((), ())), preferred_element_type=F32)
    from_look[...] = turned_look.astype(BF16)

    mine_forward.wait()
    wait_bytes(rows_of(landed, SLOTS - CAP2), recv_sem.at[1])
    came = split3(landed[...])
    sums = jnp.dot(same_row, came, preferred_element_type=F32)
    slot_grads = sums[:, :WIDTH] + (sums[:, WIDTH : 2 * WIDTH] + sums[:, 2 * WIDTH :])
    slot_accum = old_accum + jnp.mean(slot_grads * slot_grads, axis=1, keepdims=True)
    fresh_slots = old_rows - learn_rate * slot_grads / jnp.sqrt(slot_accum)
    picked[...] = fresh_slots.astype(BF16).reshape(GROUPS, CAP2, WIDTH)
    mine_picked = exchange(picked, returned, 2, FROM_NEAR)

    turned = jnp.transpose(jnp.concatenate([accum[...]] * (WIDTH // 8), axis=0))
    next_accum = jnp.zeros((WIDTH, WIDTH), F32)
    lane = iota((WIDTH, WIDTH), 1)
    for a in range(ROWS // WIDTH):
        part = slice(a * WIDTH, (a + 1) * WIDTH)
        sums = jnp.dot(to_row[part], came, preferred_element_type=F32)
        row_grads = sums[:, :WIDTH] + (sums[:, WIDTH : 2 * WIDTH] + sums[:, 2 * WIDTH :])
        row_accum = turned[:, a : a + 1] + jnp.mean(row_grads * row_grads, axis=1, keepdims=True)
        new_table[part, :] = table[part, :] - learn_rate * row_grads / jnp.sqrt(row_accum)
        next_accum = jnp.where(lane == a, row_accum, next_accum)
    new_accum[...] = jnp.transpose(next_accum)[: ROWS // WIDTH]

    mine_picked.wait()
    wait_bytes(rows_of(returned, GROUPS - 1), recv_sem.at[2])
    gathered = jnp.dot(from_group, returned[...].reshape(SLOTS, WIDTH), preferred_element_type=F32)
    back[...] = gathered.astype(BF16).reshape(MEMBERS, PAD1, WIDTH)
    for p in node_peers:
        pltpu.make_async_remote_copy(
            back.at[p], reached.at[n], send_sem.at[3], recv_sem.at[3], device_id={"node": p}, device_id_type=MESH
        ).start()
    reached[n] = back[n]

    landing = reached.at[pl.ds(0, MEMBERS - 1)]
    wait_bytes(landing, recv_sem.at[3])

    wait_bytes(routed.at[pl.ds(0, MEMBERS - 1)], send_sem.at[0])
    wait_bytes(rows_of(forwarded, SLOTS - CAP2), send_sem.at[1])
    wait_bytes(rows_of(picked, GROUPS - 1), send_sem.at[2])
    wait_bytes(back.at[pl.ds(0, MEMBERS - 1)], send_sem.at[3])


def hand_over(table, accum, from_look, reached, table_out, accum_out, fresh_out, fresh, sem):
    copies = [
        pltpu.make_async_copy(source, target, sem.at[i])
        for i, (source, target) in enumerate(((table, table_out), (accum, accum_out), (fresh, fresh_out)))
    ]
    copies[0].start()
    copies[1].start()
    read = jnp.dot(from_look[...], reached[...].reshape(MEMBERS * PAD1, WIDTH), preferred_element_type=F32)
    fresh[...] = read.astype(BF16)
    copies[2].start()
    for copy in copies:
        copy.wait()


def on_device(bag_grads, bag_lengths, look_slot, group_slot, owner_row, table, accum):
    outs = pl.pallas_call(
        kernel,
        out_shape=(
            jax.ShapeDtypeStruct((ROWS, WIDTH), F32),
            jax.ShapeDtypeStruct((ROWS // WIDTH, WIDTH), F32),
            jax.ShapeDtypeStruct((LOOKS, MEMBERS * PAD1), BF16),
            jax.ShapeDtypeStruct((MEMBERS, PAD1, WIDTH), BF16),
        ),
        in_specs=[pl.BlockSpec(memory_space=pltpu.HBM)] * 7,
        out_specs=[pl.BlockSpec(memory_space=pltpu.VMEM)] * 4,
        scratch_shapes=[
            pltpu.VMEM((BAGS, WIDTH), F32),
            pltpu.VMEM((1, BAGS), jnp.int32),
            pltpu.VMEM((1, LOOKS), jnp.int32),
            pltpu.VMEM((1, MEMBERS, CAP1), jnp.int32),
            pltpu.VMEM((1, CAP2, GROUPS), jnp.int32),
            pltpu.VMEM((ROWS, WIDTH), F32),
            pltpu.VMEM((ROWS // WIDTH, WIDTH), F32),
            pltpu.VMEM((MEMBERS, CAP1, WIDTH), F32),
            pltpu.VMEM((MEMBERS, CAP1, WIDTH), F32),
            pltpu.VMEM((SLOTS, WIDTH), F32),
            pltpu.VMEM((SLOTS, WIDTH), F32),
            pltpu.VMEM((GROUPS, CAP2, WIDTH), BF16),
            pltpu.VMEM((GROUPS, CAP2, WIDTH), BF16),
            pltpu.VMEM((MEMBERS, PAD1, WIDTH), BF16),
            pltpu.SemaphoreType.DMA((7,)),
            pltpu.SemaphoreType.DMA((2,)),
            pltpu.SemaphoreType.DMA((4,)),
            pltpu.SemaphoreType.DMA((4,)),
            pltpu.SemaphoreType.REGULAR,
        ],
        compiler_params=pltpu.CompilerParams(collective_id=0, has_side_effects=True, vmem_limit_bytes=32 * 1024 * 1024),
        cost_estimate=pl.CostEstimate(flops=600_000_000, bytes_accessed=1_400_000, transcendentals=1024),
    )(
        *[pltpu.with_memory_space_constraint(a, pltpu.HBM) for a in (bag_grads, bag_lengths, look_slot, group_slot, jnp.transpose(owner_row, (0, 2, 1)), table, accum.reshape(ROWS // WIDTH, WIDTH))]
    )
    table, accum, fresh = pl.pallas_call(
        hand_over,
        out_shape=[
            jax.ShapeDtypeStruct((ROWS, WIDTH), F32),
            jax.ShapeDtypeStruct((ROWS // WIDTH, WIDTH), F32),
            jax.ShapeDtypeStruct((LOOKS, WIDTH), BF16),
        ],
        in_specs=[pl.BlockSpec(memory_space=pltpu.VMEM)] * 4,
        out_specs=[pl.BlockSpec(memory_space=pltpu.HBM)] * 3,
        scratch_shapes=[pltpu.VMEM((LOOKS, WIDTH), BF16), pltpu.SemaphoreType.DMA((3,))],
        compiler_params=pltpu.CompilerParams(vmem_limit_bytes=16 * 1024 * 1024),
        cost_estimate=pl.CostEstimate(flops=0, bytes_accessed=1_400_000, transcendentals=0),
    )(*outs)
    return table, accum.reshape(ROWS), fresh


def solution(mesh):
    both = ("outer", "node")
    placed = (
        P(both, None),
        P(both, None),
        P(both, None),
        P(both, None, None),
        P(both, None, None),
        P(both, None),
        P(both),
    )
    return jax.shard_map(
        on_device,
        mesh=mesh,
        in_specs=placed,
        out_specs=(P(both, None), P(both), P(both, None)),
        check_vma=False,
    )
```

```python
import functools

import jax
import jax.numpy as jnp
from jax import lax
from jax.experimental import pallas as pl
from jax.experimental.pallas import tpu as pltpu
from jax.sharding import PartitionSpec as P

learn_rate = 0.3
MESH = pl.DeviceIdType.MESH
GROUPS = 96
FROM_FAR = (6, 5, 7, 4, 8, 3, 9, 2, 10, 1, 11, 0)
FROM_NEAR = (0, 1, 2, 3, 4, 5, 6, 7, 8, 9, 10, 11)
PLANES = 12
SIDES = 8
MEMBERS = 8
CAP1 = 24
PAD1 = 32
CAP2 = 2
ROWS = 1024
LOOKS = 512
BAGS = 32
WIDTH = 128
SLOTS = 192
F32 = jnp.float32
BF16 = jnp.bfloat16


def iota(shape, dim):
    return lax.broadcasted_iota(jnp.int32, shape, dim)


def hot(condition):
    return jnp.where(condition, 1.0, 0.0).astype(BF16)


def split3(value):
    high = value.astype(BF16)
    rest = value - high.astype(F32)
    middle = rest.astype(BF16)
    low = (rest - middle.astype(F32)).astype(BF16)
    return jnp.concatenate([high, middle, low], axis=1)


def mix(ones, value):
    parts = jnp.dot(ones, split3(value), preferred_element_type=F32)
    return parts[:, :WIDTH] + (parts[:, WIDTH : 2 * WIDTH] + parts[:, 2 * WIDTH :])


def kernel(
    grads_in,
    lengths_in,
    look_in,
    group_in,
    owner_in,
    table_in,
    accum_in,
    new_table,
    new_accum,
    from_look,
    reached,
    grads,
    lengths,
    look,
    group,
    owner,
    table,
    accum,
    routed,
    arrived,
    forwarded,
    landed,
    picked,
    returned,
    back,
    load_sem,
    own_sem,
    send_sem,
    recv_sem,
    side_sem,
):
    o = lax.axis_index("outer")
    n = lax.axis_index("node")
    z = o // SIDES
    side = lax.rem(o, SIDES)
    loads = [
        pltpu.make_async_copy(source, target, load_sem.at[i])
        for i, (source, target) in enumerate(
            (
                (look_in, look),
                (lengths_in, lengths),
                (grads_in, grads),
                (group_in, group),
                (owner_in, owner),
                (accum_in, accum),
                (table_in, table),
            )
        )
    ]
    for load in loads:
        load.start()

    barrier = pltpu.get_barrier_semaphore()
    node_peers = [lax.rem(n + i, MEMBERS) for i in (4, 3, 5, 2, 6, 1, 7)]
    plane_peers = [lax.rem(z + i, PLANES) * SIDES + side for i in (6, 5, 7, 4, 8, 3, 9, 2, 10, 1, 11)]
    side_peers = [z * SIDES + lax.rem(side + i, SIDES) for i in (4, 3, 5, 2, 6, 1, 7)]
    for p in node_peers:
        pl.semaphore_signal(barrier, 1, device_id={"node": p}, device_id_type=MESH)
    for p in plane_peers:
        pl.semaphore_signal(barrier, 1, device_id={"outer": p}, device_id_type=MESH)
    for p in side_peers:
        pl.semaphore_signal(barrier, 1, device_id={"outer": p}, device_id_type=MESH)

    loads[0].wait()
    loads[1].wait()
    loads[2].wait()
    before = jnp.where(iota((BAGS, BAGS), 1) <= iota((BAGS, BAGS), 0), lengths[...], 0)
    ends = jnp.sum(before, axis=1, keepdims=True)
    own = jnp.where(iota((BAGS, BAGS), 1) == iota((BAGS, BAGS), 0), lengths[...], 0)
    starts = ends - jnp.sum(own, axis=1, keepdims=True)
    place = iota((BAGS, LOOKS), 1)
    of_bag = hot((place >= starts) & (place < ends))
    of_slot = hot(iota((SLOTS, LOOKS), 0) == look[...])
    counts = lax.dot_general(of_slot, of_bag, (((1,), (1,)), ((), ())), preferred_element_type=F32)
    routed[...] = mix(counts.astype(BF16), grads[...]).reshape(MEMBERS, CAP1, WIDTH)

    pl.semaphore_wait(barrier, MEMBERS - 1 + PLANES - 1 + SIDES - 1)
    for p in node_peers:
        pltpu.make_async_remote_copy(
            routed.at[p], arrived.at[n], send_sem.at[0], recv_sem.at[0], device_id={"node": p}, device_id_type=MESH
        ).start()
    for p in side_peers:
        pl.semaphore_signal(side_sem, 1, device_id={"outer": p}, device_id_type=MESH)
    arrived[n] = routed[n]

    loads[3].wait()
    sender = lax.shift_right_logical(iota((MEMBERS, SLOTS), 1) * 2731, 16)
    column = lax.shift_right_logical(iota((CAP1, SLOTS), 1) * 2731, 16)
    spread = hot(iota((CAP1, SLOTS), 1) - CAP1 * column == iota((CAP1, SLOTS), 0))
    slots = jnp.dot(group[0].astype(F32).astype(BF16), spread, preferred_element_type=F32)
    group_row = jnp.sum(jnp.where(sender == iota((MEMBERS, SLOTS), 0), slots, 0.0), axis=0, keepdims=True).astype(jnp.int32)
    to_group = hot(iota((SLOTS, SLOTS), 0) == group_row)

    landing = arrived.at[pl.ds(0, MEMBERS - 1)]
    pltpu.make_async_copy(landing, landing, recv_sem.at[0]).wait()
    forwarded[...] = mix(to_group, arrived[...].reshape(SLOTS, WIDTH))
    pl.semaphore_wait(side_sem, SIDES - 1)

    def exchange(source, target, index, order):
        for place_z in order:
            plane = place_z * SIDES

            def send(i, carry, plane=plane):
                p = plane + lax.rem(side + i, SIDES)
                pltpu.make_async_remote_copy(
                    source.at[pl.ds(CAP2 * p, CAP2)],
                    target.at[pl.ds(CAP2 * o, CAP2)],
                    send_sem.at[index],
                    recv_sem.at[index],
                    device_id={"outer": p},
                    device_id_type=MESH,
                ).start()
                return carry

            lax.fori_loop(1, SIDES, send, 0, unroll=7)

            @pl.when(z != place_z)
            def _(plane=plane, send=send):
                send(0, 0)
        mine = pltpu.make_async_copy(
            source.at[pl.ds(CAP2 * o, CAP2)], target.at[pl.ds(CAP2 * o, CAP2)], own_sem.at[index - 1]
        )
        mine.start()
        return mine

    def rows_of(ref, rows):
        return ref.at[pl.ds(0, rows)]

    def wait_bytes(part, semaphore):
        pltpu.make_async_copy(part, part, semaphore).wait()

    mine_forward = exchange(forwarded, landed, 1, FROM_FAR)

    loads[4].wait()
    loads[5].wait()
    loads[6].wait()
    owner_high = lax.shift_right_logical(owner[0], 5)
    owner_low = owner[0] - 32 * owner_high
    digits = jnp.concatenate([owner_high, owner_low], axis=0).astype(F32).astype(BF16)
    pair = hot(lax.shift_right_logical(iota((GROUPS, SLOTS), 1), 1) == iota((GROUPS, SLOTS), 0))
    laid = jnp.dot(digits, pair, preferred_element_type=F32)
    even = (iota((1, SLOTS), 1) & 1) == 0
    owner_row = 32.0 * jnp.where(even, laid[0:1], laid[1:2]) + jnp.where(even, laid[2:3], laid[3:4])
    owner_row = owner_row.astype(jnp.int32)
    diagonal = iota((SLOTS, SLOTS), 0) == iota((SLOTS, SLOTS), 1)
    owner_column = jnp.sum(jnp.where(diagonal, owner_row, 0), axis=1, keepdims=True)
    same_row = hot(owner_column == owner_row)
    to_row = hot(iota((ROWS, SLOTS), 0) == owner_row)
    from_row = hot(owner_column == iota((SLOTS, ROWS), 1))
    old_rows = mix(from_row, table[...])
    by_lane = jnp.where((owner_column & 127) == iota((SLOTS, WIDTH), 1), 1.0, 0.0)
    by_block = lax.shift_right_logical(owner_column, 7)
    chosen = jnp.zeros((SLOTS, WIDTH), F32)
    for a in range(ROWS // WIDTH):
        chosen = jnp.where(by_block == a, accum[a : a + 1, :], chosen)
    old_accum = jnp.sum(chosen * by_lane, axis=1, keepdims=True)

    padded = iota((MEMBERS * PAD1, SLOTS), 0)
    slot_place = iota((MEMBERS * PAD1, SLOTS), 1)
    spaced = hot(slot_place + 8 * lax.shift_right_logical(slot_place * 2731, 16) == padded)
    from_group = lax.dot_general(spaced, to_group, (((1,), (1,)), ((), ())), preferred_element_type=F32).astype(BF16)
    look_spaced = look[...] + 8 * lax.shift_right_logical(look[...] * 2731, 16)
    look_hot = hot(iota((MEMBERS * PAD1, LOOKS), 0) == look_spaced)
    eye = hot(iota((LOOKS, LOOKS), 0) == iota((LOOKS, LOOKS), 1))
    turned_look = lax.dot_general(eye, look_hot, (((1,), (1,)), ((), ())), preferred_element_type=F32)
    from_look[...] = turned_look.astype(BF16)

    mine_forward.wait()
    wait_bytes(rows_of(landed, SLOTS - CAP2), recv_sem.at[1])
    came = split3(landed[...])
    sums = jnp.dot(same_row, came, preferred_element_type=F32)
    slot_grads = sums[:, :WIDTH] + (sums[:, WIDTH : 2 * WIDTH] + sums[:, 2 * WIDTH :])
    slot_accum = old_accum + jnp.mean(slot_grads * slot_grads, axis=1, keepdims=True)
    fresh_slots = old_rows - learn_rate * slot_grads / jnp.sqrt(slot_accum)
    picked[...] = fresh_slots.astype(BF16).astype(F32)
    mine_picked = exchange(picked, returned, 2, FROM_NEAR)

    turned = jnp.transpose(jnp.concatenate([accum[...]] * (WIDTH // 8), axis=0))
    next_accum = jnp.zeros((WIDTH, WIDTH), F32)
    lane = iota((WIDTH, WIDTH), 1)
    for a in range(ROWS // WIDTH):
        part = slice(a * WIDTH, (a + 1) * WIDTH)
        sums = jnp.dot(to_row[part], came, preferred_element_type=F32)
        row_grads = sums[:, :WIDTH] + (sums[:, WIDTH : 2 * WIDTH] + sums[:, 2 * WIDTH :])
        row_accum = turned[:, a : a + 1] + jnp.mean(row_grads * row_grads, axis=1, keepdims=True)
        new_table[part, :] = table[part, :] - learn_rate * row_grads / jnp.sqrt(row_accum)
        next_accum = jnp.where(lane == a, row_accum, next_accum)
    new_accum[...] = jnp.transpose(next_accum)[: ROWS // WIDTH]

    mine_picked.wait()
    wait_bytes(rows_of(returned, SLOTS - CAP2), recv_sem.at[2])
    gathered = jnp.dot(from_group, returned[...].astype(BF16), preferred_element_type=F32)
    back[...] = gathered.astype(BF16).reshape(MEMBERS, PAD1, WIDTH)
    for p in node_peers:
        pltpu.make_async_remote_copy(
            back.at[p], reached.at[n], send_sem.at[3], recv_sem.at[3], device_id={"node": p}, device_id_type=MESH
        ).start()
    reached[n] = back[n]

    landing = reached.at[pl.ds(0, MEMBERS - 1)]
    wait_bytes(landing, recv_sem.at[3])

    wait_bytes(routed.at[pl.ds(0, MEMBERS - 1)], send_sem.at[0])
    wait_bytes(rows_of(forwarded, SLOTS - CAP2), send_sem.at[1])
    wait_bytes(rows_of(picked, SLOTS - CAP2), send_sem.at[2])
    wait_bytes(back.at[pl.ds(0, MEMBERS - 1)], send_sem.at[3])


def hand_over(table, accum, from_look, reached, table_out, accum_out, fresh_out, fresh, sem):
    copies = [
        pltpu.make_async_copy(source, target, sem.at[i])
        for i, (source, target) in enumerate(((table, table_out), (accum, accum_out), (fresh, fresh_out)))
    ]
    copies[0].start()
    copies[1].start()
    read = jnp.dot(from_look[...], reached[...].reshape(MEMBERS * PAD1, WIDTH), preferred_element_type=F32)
    fresh[...] = read.astype(BF16)
    copies[2].start()
    for copy in copies:
        copy.wait()


def on_device(bag_grads, bag_lengths, look_slot, group_slot, owner_row, table, accum):
    outs = pl.pallas_call(
        kernel,
        out_shape=(
            jax.ShapeDtypeStruct((ROWS, WIDTH), F32),
            jax.ShapeDtypeStruct((ROWS // WIDTH, WIDTH), F32),
            jax.ShapeDtypeStruct((LOOKS, MEMBERS * PAD1), BF16),
            jax.ShapeDtypeStruct((MEMBERS, PAD1, WIDTH), BF16),
        ),
        in_specs=[pl.BlockSpec(memory_space=pltpu.HBM)] * 7,
        out_specs=[pl.BlockSpec(memory_space=pltpu.VMEM)] * 4,
        scratch_shapes=[
            pltpu.VMEM((BAGS, WIDTH), F32),
            pltpu.VMEM((1, BAGS), jnp.int32),
            pltpu.VMEM((1, LOOKS), jnp.int32),
            pltpu.VMEM((1, MEMBERS, CAP1), jnp.int32),
            pltpu.VMEM((1, CAP2, GROUPS), jnp.int32),
            pltpu.VMEM((ROWS, WIDTH), F32),
            pltpu.VMEM((ROWS // WIDTH, WIDTH), F32),
            pltpu.VMEM((MEMBERS, CAP1, WIDTH), F32),
            pltpu.VMEM((MEMBERS, CAP1, WIDTH), F32),
            pltpu.VMEM((SLOTS, WIDTH), F32),
            pltpu.VMEM((SLOTS, WIDTH), F32),
            pltpu.VMEM((SLOTS, WIDTH), F32),
            pltpu.VMEM((SLOTS, WIDTH), F32),
            pltpu.VMEM((MEMBERS, PAD1, WIDTH), BF16),
            pltpu.SemaphoreType.DMA((7,)),
            pltpu.SemaphoreType.DMA((2,)),
            pltpu.SemaphoreType.DMA((4,)),
            pltpu.SemaphoreType.DMA((4,)),
            pltpu.SemaphoreType.REGULAR,
        ],
        compiler_params=pltpu.CompilerParams(collective_id=0, has_side_effects=True, vmem_limit_bytes=32 * 1024 * 1024),
        cost_estimate=pl.CostEstimate(flops=600_000_000, bytes_accessed=1_400_000, transcendentals=1024),
    )(
        *[pltpu.with_memory_space_constraint(a, pltpu.HBM) for a in (bag_grads, bag_lengths, look_slot, group_slot, jnp.transpose(owner_row, (0, 2, 1)), table, accum.reshape(ROWS // WIDTH, WIDTH))]
    )
    table, accum, fresh = pl.pallas_call(
        hand_over,
        out_shape=[
            jax.ShapeDtypeStruct((ROWS, WIDTH), F32),
            jax.ShapeDtypeStruct((ROWS // WIDTH, WIDTH), F32),
            jax.ShapeDtypeStruct((LOOKS, WIDTH), BF16),
        ],
        in_specs=[pl.BlockSpec(memory_space=pltpu.VMEM)] * 4,
        out_specs=[pl.BlockSpec(memory_space=pltpu.HBM)] * 3,
        scratch_shapes=[pltpu.VMEM((LOOKS, WIDTH), BF16), pltpu.SemaphoreType.DMA((3,))],
        compiler_params=pltpu.CompilerParams(vmem_limit_bytes=16 * 1024 * 1024),
        cost_estimate=pl.CostEstimate(flops=0, bytes_accessed=1_400_000, transcendentals=0),
    )(*outs)
    return table, accum.reshape(ROWS), fresh


def solution(mesh):
    both = ("outer", "node")
    placed = (
        P(both, None),
        P(both, None),
        P(both, None),
        P(both, None, None),
        P(both, None, None),
        P(both, None),
        P(both),
    )
    return jax.shard_map(
        on_device,
        mesh=mesh,
        in_specs=placed,
        out_specs=(P(both, None), P(both), P(both, None)),
        check_vma=False,
    )
```

```python
import functools

import jax
import jax.numpy as jnp
from jax import lax
from jax.experimental import pallas as pl
from jax.experimental.pallas import tpu as pltpu
from jax.sharding import PartitionSpec as P

learn_rate = 0.3
MESH = pl.DeviceIdType.MESH
GROUPS = 96
FROM_FAR = (6, 5, 7, 4, 8, 3, 9, 2, 10, 1, 11, 0)
FROM_NEAR = (0, 1, 2, 3, 4, 5, 6, 7, 8, 9, 10, 11)
PLANES = 12
SIDES = 8
MEMBERS = 8
CAP1 = 24
PAD1 = 32
CAP2 = 2
ROWS = 1024
LOOKS = 512
BAGS = 32
WIDTH = 128
SLOTS = 192
F32 = jnp.float32
BF16 = jnp.bfloat16


def iota(shape, dim):
    return lax.broadcasted_iota(jnp.int32, shape, dim)


def hot(condition):
    return jnp.where(condition, 1.0, 0.0).astype(BF16)


def split3(value):
    high = value.astype(BF16)
    rest = value - high.astype(F32)
    middle = rest.astype(BF16)
    low = (rest - middle.astype(F32)).astype(BF16)
    return jnp.concatenate([high, middle, low], axis=1)


def mix(ones, value):
    parts = jnp.dot(ones, split3(value), preferred_element_type=F32)
    return parts[:, :WIDTH] + (parts[:, WIDTH : 2 * WIDTH] + parts[:, 2 * WIDTH :])


def kernel(
    grads_in,
    lengths_in,
    look_in,
    group_in,
    owner_in,
    table_in,
    accum_in,
    new_table,
    new_accum,
    from_look,
    reached,
    grads,
    lengths,
    look,
    group,
    owner,
    table,
    accum,
    routed,
    arrived,
    forwarded,
    landed,
    picked,
    returned,
    back,
    load_sem,
    own_sem,
    send_sem,
    recv_sem,
    side_sem,
):
    o = lax.axis_index("outer")
    n = lax.axis_index("node")
    z = o // SIDES
    side = lax.rem(o, SIDES)
    loads = [
        pltpu.make_async_copy(source, target, load_sem.at[i])
        for i, (source, target) in enumerate(
            (
                (look_in, look),
                (lengths_in, lengths),
                (grads_in, grads),
                (group_in, group),
                (owner_in, owner),
                (accum_in, accum),
                (table_in, table),
            )
        )
    ]
    for load in loads:
        load.start()

    barrier = pltpu.get_barrier_semaphore()
    node_peers = [lax.rem(n + i, MEMBERS) for i in (4, 3, 5, 2, 6, 1, 7)]
    plane_peers = [lax.rem(z + i, PLANES) * SIDES + side for i in (6, 5, 7, 4, 8, 3, 9, 2, 10, 1, 11)]
    side_peers = [z * SIDES + lax.rem(side + i, SIDES) for i in (4, 3, 5, 2, 6, 1, 7)]
    for p in node_peers:
        pl.semaphore_signal(barrier, 1, device_id={"node": p}, device_id_type=MESH)
    for p in plane_peers:
        pl.semaphore_signal(barrier, 1, device_id={"outer": p}, device_id_type=MESH)
    for p in side_peers:
        pl.semaphore_signal(barrier, 1, device_id={"outer": p}, device_id_type=MESH)

    loads[0].wait()
    loads[1].wait()
    loads[2].wait()
    before = jnp.where(iota((BAGS, BAGS), 1) <= iota((BAGS, BAGS), 0), lengths[...], 0)
    ends = jnp.sum(before, axis=1, keepdims=True)
    own = jnp.where(iota((BAGS, BAGS), 1) == iota((BAGS, BAGS), 0), lengths[...], 0)
    starts = ends - jnp.sum(own, axis=1, keepdims=True)
    place = iota((BAGS, LOOKS), 1)
    of_bag = hot((place >= starts) & (place < ends))
    of_slot = hot(iota((SLOTS, LOOKS), 0) == look[...])
    counts = lax.dot_general(of_slot, of_bag, (((1,), (1,)), ((), ())), preferred_element_type=F32)
    routed[...] = mix(counts.astype(BF16), grads[...]).reshape(MEMBERS, CAP1, WIDTH)

    pl.semaphore_wait(barrier, MEMBERS - 1 + PLANES - 1 + SIDES - 1)
    for p in node_peers:
        pltpu.make_async_remote_copy(
            routed.at[p], arrived.at[n], send_sem.at[0], recv_sem.at[0], device_id={"node": p}, device_id_type=MESH
        ).start()
    for p in side_peers:
        pl.semaphore_signal(side_sem, 1, device_id={"outer": p}, device_id_type=MESH)
    arrived[n] = routed[n]

    loads[3].wait()
    sender = lax.shift_right_logical(iota((MEMBERS, SLOTS), 1) * 2731, 16)
    column = lax.shift_right_logical(iota((CAP1, SLOTS), 1) * 2731, 16)
    spread = hot(iota((CAP1, SLOTS), 1) - CAP1 * column == iota((CAP1, SLOTS), 0))
    slots = jnp.dot(group[0].astype(F32).astype(BF16), spread, preferred_element_type=F32)
    group_row = jnp.sum(jnp.where(sender == iota((MEMBERS, SLOTS), 0), slots, 0.0), axis=0, keepdims=True).astype(jnp.int32)
    to_group = hot(iota((SLOTS, SLOTS), 0) == group_row)

    landing = arrived.at[pl.ds(0, MEMBERS - 1)]
    pltpu.make_async_copy(landing, landing, recv_sem.at[0]).wait()
    forwarded[...] = mix(to_group, arrived[...].reshape(SLOTS, WIDTH))
    pl.semaphore_wait(side_sem, SIDES - 1)

    def block(ref, group):
        return ref.at[pl.ds(CAP2 * group, CAP2)] if len(ref.shape) == 2 else ref.at[group]

    def exchange(source, target, index, order):
        for place_z in order:
            plane = place_z * SIDES

            def send(i, carry, plane=plane):
                p = plane + lax.rem(side + i, SIDES)
                pltpu.make_async_remote_copy(
                    block(source, p),
                    block(target, o),
                    send_sem.at[index],
                    recv_sem.at[index],
                    device_id={"outer": p},
                    device_id_type=MESH,
                ).start()
                return carry

            for i in (4, 5, 3, 6, 7, 2, 1):
                send(i, 0)

            @pl.when(z != place_z)
            def _(plane=plane, send=send):
                send(0, 0)
        mine = pltpu.make_async_copy(
            block(source, o), block(target, o), own_sem.at[index - 1]
        )
        mine.start()
        return mine

    def rows_of(ref, rows):
        return ref.at[pl.ds(0, rows)]

    def wait_bytes(part, semaphore):
        pltpu.make_async_copy(part, part, semaphore).wait()

    mine_forward = exchange(forwarded, landed, 1, FROM_FAR)

    loads[4].wait()
    loads[5].wait()
    loads[6].wait()
    owner_high = lax.shift_right_logical(owner[0], 5)
    owner_low = owner[0] - 32 * owner_high
    digits = jnp.concatenate([owner_high, owner_low], axis=0).astype(F32).astype(BF16)
    pair = hot(lax.shift_right_logical(iota((GROUPS, SLOTS), 1), 1) == iota((GROUPS, SLOTS), 0))
    laid = jnp.dot(digits, pair, preferred_element_type=F32)
    even = (iota((1, SLOTS), 1) & 1) == 0
    owner_row = 32.0 * jnp.where(even, laid[0:1], laid[1:2]) + jnp.where(even, laid[2:3], laid[3:4])
    owner_row = owner_row.astype(jnp.int32)
    diagonal = iota((SLOTS, SLOTS), 0) == iota((SLOTS, SLOTS), 1)
    owner_column = jnp.sum(jnp.where(diagonal, owner_row, 0), axis=1, keepdims=True)
    same_row = hot(owner_column == owner_row)
    to_row = hot(iota((ROWS, SLOTS), 0) == owner_row)
    from_row = hot(owner_column == iota((SLOTS, ROWS), 1))
    old_rows = mix(from_row, table[...])
    by_lane = jnp.where((owner_column & 127) == iota((SLOTS, WIDTH), 1), 1.0, 0.0)
    by_block = lax.shift_right_logical(owner_column, 7)
    chosen = jnp.zeros((SLOTS, WIDTH), F32)
    for a in range(ROWS // WIDTH):
        chosen = jnp.where(by_block == a, accum[a : a + 1, :], chosen)
    old_accum = jnp.sum(chosen * by_lane, axis=1, keepdims=True)

    padded = iota((MEMBERS * PAD1, SLOTS), 0)
    slot_place = iota((MEMBERS * PAD1, SLOTS), 1)
    spaced = hot(slot_place + 8 * lax.shift_right_logical(slot_place * 2731, 16) == padded)
    from_group = lax.dot_general(spaced, to_group, (((1,), (1,)), ((), ())), preferred_element_type=F32).astype(BF16)
    look_spaced = look[...] + 8 * lax.shift_right_logical(look[...] * 2731, 16)
    look_hot = hot(iota((MEMBERS * PAD1, LOOKS), 0) == look_spaced)
    eye = hot(iota((LOOKS, LOOKS), 0) == iota((LOOKS, LOOKS), 1))
    turned_look = lax.dot_general(eye, look_hot, (((1,), (1,)), ((), ())), preferred_element_type=F32)
    from_look[...] = turned_look.astype(BF16)

    mine_forward.wait()
    wait_bytes(rows_of(landed, SLOTS - CAP2), recv_sem.at[1])
    came = split3(landed[...])
    sums = jnp.dot(same_row, came, preferred_element_type=F32)
    slot_grads = sums[:, :WIDTH] + (sums[:, WIDTH : 2 * WIDTH] + sums[:, 2 * WIDTH :])
    slot_accum = old_accum + jnp.mean(slot_grads * slot_grads, axis=1, keepdims=True)
    fresh_slots = old_rows - learn_rate * slot_grads / jnp.sqrt(slot_accum)
    picked[...] = fresh_slots.astype(BF16).reshape(GROUPS, CAP2, WIDTH)
    mine_picked = exchange(picked, returned, 2, FROM_NEAR)

    turned = jnp.transpose(jnp.concatenate([accum[...]] * (WIDTH // 8), axis=0))
    next_accum = jnp.zeros((WIDTH, WIDTH), F32)
    lane = iota((WIDTH, WIDTH), 1)
    for a in range(ROWS // WIDTH):
        part = slice(a * WIDTH, (a + 1) * WIDTH)
        sums = jnp.dot(to_row[part], came, preferred_element_type=F32)
        row_grads = sums[:, :WIDTH] + (sums[:, WIDTH : 2 * WIDTH] + sums[:, 2 * WIDTH :])
        row_accum = turned[:, a : a + 1] + jnp.mean(row_grads * row_grads, axis=1, keepdims=True)
        new_table[part, :] = table[part, :] - learn_rate * row_grads / jnp.sqrt(row_accum)
        next_accum = jnp.where(lane == a, row_accum, next_accum)
    new_accum[...] = jnp.transpose(next_accum)[: ROWS // WIDTH]

    mine_picked.wait()
    wait_bytes(rows_of(returned, GROUPS - 1), recv_sem.at[2])
    came_back = returned[...].reshape(SLOTS, WIDTH)

    def give(p):
        pltpu.make_async_remote_copy(
            back.at[p], reached.at[n], send_sem.at[3], recv_sem.at[3], device_id={"node": p}, device_id_type=MESH
        ).start()

    first = jnp.dot(from_group[:PAD1], came_back, preferred_element_type=F32)
    back[0] = first.astype(BF16)

    @pl.when(n != 0)
    def _():
        give(0)

    gathered = jnp.dot(from_group[PAD1:], came_back, preferred_element_type=F32)
    back[1:] = gathered.astype(BF16).reshape(MEMBERS - 1, PAD1, WIDTH)
    for p in node_peers:

        @pl.when(p != 0)
        def _(p=p):
            give(p)

    reached[n] = back[n]

    landing = reached.at[pl.ds(0, MEMBERS - 1)]
    wait_bytes(landing, recv_sem.at[3])

    wait_bytes(routed.at[pl.ds(0, MEMBERS - 1)], send_sem.at[0])
    wait_bytes(rows_of(forwarded, SLOTS - CAP2), send_sem.at[1])
    wait_bytes(rows_of(picked, GROUPS - 1), send_sem.at[2])
    wait_bytes(back.at[pl.ds(0, MEMBERS - 1)], send_sem.at[3])


def hand_over(table, accum, from_look, reached, table_out, accum_out, fresh_out, fresh, sem):
    copies = [
        pltpu.make_async_copy(source, target, sem.at[i])
        for i, (source, target) in enumerate(((table, table_out), (accum, accum_out), (fresh, fresh_out)))
    ]
    copies[0].start()
    copies[1].start()
    read = jnp.dot(from_look[...], reached[...].reshape(MEMBERS * PAD1, WIDTH), preferred_element_type=F32)
    fresh[...] = read.astype(BF16)
    copies[2].start()
    for copy in copies:
        copy.wait()


def on_device(bag_grads, bag_lengths, look_slot, group_slot, owner_row, table, accum):
    outs = pl.pallas_call(
        kernel,
        out_shape=(
            jax.ShapeDtypeStruct((ROWS, WIDTH), F32),
            jax.ShapeDtypeStruct((ROWS // WIDTH, WIDTH), F32),
            jax.ShapeDtypeStruct((LOOKS, MEMBERS * PAD1), BF16),
            jax.ShapeDtypeStruct((MEMBERS, PAD1, WIDTH), BF16),
        ),
        in_specs=[pl.BlockSpec(memory_space=pltpu.HBM)] * 7,
        out_specs=[pl.BlockSpec(memory_space=pltpu.VMEM)] * 4,
        scratch_shapes=[
            pltpu.VMEM((BAGS, WIDTH), F32),
            pltpu.VMEM((1, BAGS), jnp.int32),
            pltpu.VMEM((1, LOOKS), jnp.int32),
            pltpu.VMEM((1, MEMBERS, CAP1), jnp.int32),
            pltpu.VMEM((1, CAP2, GROUPS), jnp.int32),
            pltpu.VMEM((ROWS, WIDTH), F32),
            pltpu.VMEM((ROWS // WIDTH, WIDTH), F32),
            pltpu.VMEM((MEMBERS, CAP1, WIDTH), F32),
            pltpu.VMEM((MEMBERS, CAP1, WIDTH), F32),
            pltpu.VMEM((SLOTS, WIDTH), F32),
            pltpu.VMEM((SLOTS, WIDTH), F32),
            pltpu.VMEM((GROUPS, CAP2, WIDTH), BF16),
            pltpu.VMEM((GROUPS, CAP2, WIDTH), BF16),
            pltpu.VMEM((MEMBERS, PAD1, WIDTH), BF16),
            pltpu.SemaphoreType.DMA((7,)),
            pltpu.SemaphoreType.DMA((2,)),
            pltpu.SemaphoreType.DMA((4,)),
            pltpu.SemaphoreType.DMA((4,)),
            pltpu.SemaphoreType.REGULAR,
        ],
        compiler_params=pltpu.CompilerParams(collective_id=0, has_side_effects=True, vmem_limit_bytes=32 * 1024 * 1024),
        cost_estimate=pl.CostEstimate(flops=600_000_000, bytes_accessed=1_400_000, transcendentals=1024),
    )(
        *[pltpu.with_memory_space_constraint(a, pltpu.HBM) for a in (bag_grads, bag_lengths, look_slot, group_slot, jnp.transpose(owner_row, (0, 2, 1)), table, accum.reshape(ROWS // WIDTH, WIDTH))]
    )
    table, accum, fresh = pl.pallas_call(
        hand_over,
        out_shape=[
            jax.ShapeDtypeStruct((ROWS, WIDTH), F32),
            jax.ShapeDtypeStruct((ROWS // WIDTH, WIDTH), F32),
            jax.ShapeDtypeStruct((LOOKS, WIDTH), BF16),
        ],
        in_specs=[pl.BlockSpec(memory_space=pltpu.VMEM)] * 4,
        out_specs=[pl.BlockSpec(memory_space=pltpu.HBM)] * 3,
        scratch_shapes=[pltpu.VMEM((LOOKS, WIDTH), BF16), pltpu.SemaphoreType.DMA((3,))],
        compiler_params=pltpu.CompilerParams(vmem_limit_bytes=16 * 1024 * 1024),
        cost_estimate=pl.CostEstimate(flops=0, bytes_accessed=1_400_000, transcendentals=0),
    )(*outs)
    return table, accum.reshape(ROWS), fresh


def solution(mesh):
    both = ("outer", "node")
    placed = (
        P(both, None),
        P(both, None),
        P(both, None),
        P(both, None, None),
        P(both, None, None),
        P(both, None),
        P(both),
    )
    return jax.shard_map(
        on_device,
        mesh=mesh,
        in_specs=placed,
        out_specs=(P(both, None), P(both), P(both, None)),
        check_vma=False,
    )
```
